32 devices in a mesh: level: 16 (over z, y, core), band: 2 (over x).
Axes of the slice: x: 2, y: 2, z: 4, core: 2. Of those that a mesh axis runs over, the one named last changes fastest.
Arguments:
- latents: float32 [16, 4, 10, 64], P('level', None, 'band'), may hold values from -18 to 18
- timesteps: int32 [16], P('level'), may hold values from 16 to 999
- fresh: float32 [1, 4, 10, 64], P(None, None, 'band'), may hold values from -6 to 6
- w_in: float32 [4, 320], replicated, may hold values from -3 to 3
- conv_first: float32 [3, 3, 320, 320], replicated, may hold values from -0.109375 to 0.109375
- conv_second: float32 [3, 3, 320, 320], replicated, may hold values from -0.109375 to 0.109375
- w_time: float32 [320, 320], replicated, may hold values from -0.3125 to 0.3125
- temporal: float32 [3, 320, 320], replicated, may hold values from -0.1875 to 0.1875
- w_out: float32 [320, 4], replicated, may hold values from -0.3125 to 0.3125
Outputs:
- queue: float32 [16, 4, 10, 64], P('level', None, 'band')
The draws below stay inside these ranges and needn't reach their ends.
All inputs are finite; a program needn't handle non-finite values.
Results may differ from the reference program's by a relative error of at most 0.0001.
Values sent between devices are 32-bit elements; how exact they have to be, the bound alone decides.
A program may use at most 128 MiB of HBM per device.

```python
import math
import jax
import jax.numpy as jnp
from jax import lax

C = 320
LAT = 4
W = 64
GROUPS = 32
ITERS = 2
NSTEPS = 1000
STRIDE = 16
H = 10
LEVELS = 16


def draw_latents(key, part):
    basis_key = jax.random.fold_in(jax.random.fold_in(key, 11), 0)
    row_scale = 1.0 + 2.0 * jnp.arange(H, dtype=jnp.float32) / max(H - 1, 1)
    basis = jnp.clip(jax.random.normal(basis_key, (LEVELS, LAT, H, W), jnp.float32), -6.0, 6.0)
    return (basis * row_scale[None, None, :, None]).astype(jnp.float32)


def touch_ends(entries, stream_key, smallest, largest):
    spot = [jax.random.randint(jax.random.fold_in(stream_key, axis), (), 0, length) for axis, length in enumerate(entries.shape)]
    widest = entries.shape.index(max(entries.shape))
    neighbour = spot[:widest] + [(spot[widest] + 1) % entries.shape[widest]] + spot[widest + 1:]
    return entries.at[tuple(spot)].set(smallest).at[tuple(neighbour)].set(largest)


def levels(key, extent, cuts, smallest, largest):
    loudness = 1.0
    for dim, shards_of in cuts:
        heights = jax.random.uniform(jax.random.fold_in(jax.random.fold_in(key, 6), dim), (shards_of,), jnp.float32, smallest / len(cuts), largest / len(cuts))
        loudness = loudness * jnp.repeat(jnp.exp(heights), extent[dim] // shards_of).reshape((-1,) + (1,) * (len(extent) - 1 - dim))
    return loudness


def scatter_about(rng, shape, width, reach, cuts=(), kind=jnp.bfloat16):
    values = width * jax.random.normal(rng, shape, jnp.float32)
    if cuts:
        values = values * levels(rng, shape, cuts, -0.22, 0.18)
    return jnp.clip(values, -reach, reach).astype(kind)


def setup_inputs(seed: int = 0) -> dict:
    splits = jax.random.split(jax.random.key(seed), 10)
    latents = draw_latents(jax.random.fold_in(splits[9], 71), 0)
    timesteps = touch_ends(jax.random.randint(splits[1], (LEVELS,), STRIDE, NSTEPS), jax.random.fold_in(splits[1], 1), STRIDE, NSTEPS - 1).astype(jnp.int32)
    fresh = scatter_about(splits[2], (ITERS - 1, LAT, H, W), 1.0, 6.0, ((2, 2),), jnp.float32)
    w_in = scatter_about(splits[3], (LAT, C), LAT ** -0.5, 3.0, (), jnp.float32)
    conv_first = scatter_about(splits[4], (3, 3, C, C), (9 * C) ** -0.5, 0.109375, (), jnp.float32)
    conv_second = scatter_about(splits[5], (3, 3, C, C), (9 * C) ** -0.5, 0.109375, (), jnp.float32)
    w_time = scatter_about(splits[6], (C, C), C ** -0.5, 0.3125, (), jnp.float32)
    temporal = scatter_about(splits[7], (3, C, C), (3 * C) ** -0.5, 0.1875, (), jnp.float32)
    w_out = scatter_about(splits[8], (C, LAT), C ** -0.5, 0.3125, (), jnp.float32)
    return dict(latents=latents, timesteps=timesteps, fresh=fresh, w_in=w_in, conv_first=conv_first, conv_second=conv_second, w_time=w_time, temporal=temporal, w_out=w_out)


EPSILON = 1e-05
HIGHEST = lax.Precision.HIGHEST

def noise_table():
    position = jnp.arange(NSTEPS, dtype=jnp.float32)
    root_beta = math.sqrt(0.00085) + position / (NSTEPS - 1) * (math.sqrt(0.012) - math.sqrt(0.00085))
    return jnp.cumprod(1.0 - root_beta * root_beta)

def time_embed(step_ids, w_time):
    half_width = w_time.shape[0] // 2
    frequency = jnp.exp(-math.log(10000.0) * jnp.arange(half_width, dtype=jnp.float32) / half_width)
    angles = step_ids.astype(jnp.float32)[:, None] * frequency[None, :]
    harmonic = jnp.concatenate([jnp.cos(angles), jnp.sin(angles)], axis=1)
    return jax.nn.silu(jnp.dot(harmonic, w_time, precision=HIGHEST, preferred_element_type=jnp.float32))

def group_norm(values):
    shape_full = values.shape
    grouped = values.reshape(shape_full[0], shape_full[1], shape_full[2], GROUPS, shape_full[3] // GROUPS)
    center = lax.optimization_barrier(jnp.mean(grouped, axis=(1, 2, 4), keepdims=True))
    spread = lax.optimization_barrier(jnp.mean(grouped * grouped, axis=(1, 2, 4), keepdims=True)) - center * center
    return ((grouped - center) * lax.rsqrt(spread + EPSILON)).reshape(shape_full)

def convolve(values, kernel):
    height = values.shape[1]
    columns = values.shape[2]
    widened = jnp.pad(values, ((0, 0), (1, 1), (1, 1), (0, 0)))
    result = jnp.zeros(values.shape[:3] + (kernel.shape[3],), jnp.float32)
    for row_tap in range(3):
        for col_tap in range(3):
            result = result + jnp.einsum('lhwc,cd->lhwd', widened[:, row_tap:row_tap + height, col_tap:col_tap + columns], kernel[row_tap, col_tap], precision=HIGHEST)
    return result

def reference(latents, timesteps, fresh, w_in, conv_first, conv_second, w_time, temporal, w_out):
    levels_all = latents.shape[0]
    latent_now = latents.transpose(0, 2, 3, 1)
    plan = noise_table()
    alpha_now = plan[timesteps.astype(jnp.int32)][:, None, None, None]
    alpha_prev = plan[(timesteps - STRIDE).astype(jnp.int32)][:, None, None, None]
    embedded = time_embed(timesteps, w_time)
    for iteration in range(ITERS):
        lifted = jnp.einsum('lhwk,kc->lhwc', latent_now, w_in, precision=HIGHEST)
        middle = convolve(jax.nn.silu(group_norm(lifted)), conv_first) + embedded[:, None, None, :]
        hidden = lifted + convolve(jax.nn.silu(group_norm(middle)), conv_second)
        activated = jax.nn.silu(group_norm(hidden))
        padded = jnp.pad(activated, ((1, 1), (0, 0), (0, 0), (0, 0)))
        blended = hidden
        for tap_index in range(3):
            blended = blended + jnp.einsum('lhwc,cd->lhwd', padded[tap_index:tap_index + levels_all], temporal[tap_index], precision=HIGHEST)
        noise_pred = jnp.einsum('lhwc,ck->lhwk', blended, w_out, precision=HIGHEST)
        denoised = (latent_now - jnp.sqrt(1.0 - alpha_now) * noise_pred) / jnp.sqrt(alpha_now)
        latent_now = jnp.sqrt(alpha_prev) * denoised + jnp.sqrt(1.0 - alpha_prev) * noise_pred
        if iteration + 1 < ITERS:
            entering = fresh[iteration].transpose(1, 2, 0)[None]
            latent_now = jnp.concatenate([entering, latent_now[:-1]], axis=0)
    return latent_now.transpose(0, 3, 1, 2)
```

```python
import functools
import math

import jax
import jax.numpy as jnp
from jax import lax
from jax.experimental import pallas as pl
from jax.experimental.pallas import tpu as pltpu
from jax.sharding import PartitionSpec as P

GROUPS = 32
ITERS = 2
NSTEPS = 1000
STRIDE = 16
EPSILON = 1e-05

MESH = pl.DeviceIdType.MESH
F32 = jnp.float32
BF16 = jnp.bfloat16
NN = (((1,), (0,)), ((), ()))
NT = (((1,), (1,)), ((), ()))
TN = (((0,), (0,)), ((), ()))


def dot(a, b, dims=NN):
    return lax.dot_general(a, b, dims, preferred_element_type=F32)


def split(v):
    high = v.astype(BF16)
    return high, (v - high.astype(F32)).astype(BF16)


def dot3(a, b, dims=NN):
    ah, al = split(a)
    bh, bl = split(b)
    return dot(ah, bh, dims) + dot(al, bh, dims) + dot(ah, bl, dims)


def silu(v):
    half = 0.5 * v
    return half + half * jnp.tanh(half)


def plan_at(step):
    rows = -(-NSTEPS // 1024) * 8
    position = lax.broadcasted_iota(jnp.int32, (rows, 128), 0) * 128
    position = position + lax.broadcasted_iota(jnp.int32, (rows, 128), 1)
    root_beta = math.sqrt(0.00085) + position.astype(F32) / (NSTEPS - 1) * (
        math.sqrt(0.012) - math.sqrt(0.00085)
    )
    kept = jnp.where(position <= step, 1.0 - root_beta * root_beta, 1.0)
    for axis, length in ((0, rows), (1, 128)):
        shift = length // 2
        while shift:
            kept = kept * pltpu.roll(kept, shift, axis)
            shift //= 2
    return kept[0:1, 0:1]


def pack_weights(raw, high_ref, low_ref, channels):
    rest = channels - 256
    high_ref[:, 3 * channels :, :] = jnp.zeros((4, 1024 - 3 * channels, 256), BF16)
    low_ref[:, 3 * channels :, :] = jnp.zeros((4, 1024 - 3 * channels, 256), BF16)
    for b in range(3):
        for n in range(4):
            if n < 3:
                piece = raw[n, b, :, 0:256]
            else:
                piece = jnp.concatenate(
                    [raw[a, b, :, 256:channels] for a in range(3)]
                    + [jnp.zeros((channels, 256 - 3 * rest), F32)],
                    axis=1,
                )
            high, low = split(piece)
            start = 768 + b * rest
            high_ref[n, b * 256 : (b + 1) * 256, :] = high[0:256]
            low_ref[n, b * 256 : (b + 1) * 256, :] = low[0:256]
            high_ref[n, start : start + rest, :] = high[256:channels]
            low_ref[n, start : start + rest, :] = low[256:channels]


def kernel(
    sizes,
    step_ref,
    pack_ref,
    small_ref,
    conv_first_hbm,
    conv_second_hbm,
    w_time_hbm,
    temporal_hbm,
    out_ref,
    raw_first,
    raw_second,
    raw_time,
    raw_temporal,
    first_high,
    first_low,
    second_high,
    second_low,
    act_high,
    act_low,
    lifted_ref,
    value_ref,
    rest_ref,
    gathered,
    send_frame,
    recv_frame,
    send_tap,
    recv_tap,
    send_last,
    recv_last,
    load_sem,
    band_send,
    band_recv,
    level_send,
    level_recv,
):
    n_level, n_band, channels, height, width, chunk = sizes
    rest = channels - 256
    pixels = height * width
    held = pixels // n_band
    block = chunk * width
    level = lax.axis_index("level")
    band = lax.axis_index("band")

    loads = [
        pltpu.make_async_copy(source, target, load_sem.at[i])
        for i, (source, target) in enumerate(
            (
                (conv_first_hbm, raw_first),
                (w_time_hbm, raw_time),
                (temporal_hbm, raw_temporal),
                (conv_second_hbm, raw_second),
            )
        )
    ]
    for load in loads:
        load.start()

    recv_frame[...] = jnp.zeros_like(recv_frame)
    recv_tap[...] = jnp.zeros_like(recv_tap)
    recv_last[...] = jnp.zeros_like(recv_last)

    has_up = level + 1 < n_level
    has_two_up = level + 2 < n_level
    has_down = level >= 1
    has_two_down = level >= 2

    barrier = pltpu.get_barrier_semaphore()
    peers = [lax.rem(band + i, n_band) for i in range(1, n_band)]

    def greet(who):
        pl.semaphore_signal(barrier, inc=1, device_id=who, device_id_type=MESH)

    for peer in peers:
        greet({"band": peer})
    pl.when(has_down)(lambda: greet({"level": level - 1}))
    pl.when(has_two_down)(lambda: greet({"level": level - 2}))
    pl.when(has_up)(lambda: greet({"level": level + 1}))
    expected = n_band - 1
    for there in (has_up, has_two_up, has_down):
        expected = expected + jnp.where(there, 1, 0)
    pl.semaphore_wait(barrier, expected)

    def band_copy(i):
        return pltpu.make_async_remote_copy(
            src_ref=pack_ref,
            dst_ref=gathered.at[i],
            send_sem=band_send.at[i],
            recv_sem=band_recv.at[i],
            device_id={"band": peers[i]},
            device_id_type=MESH,
        )

    for i in range(n_band - 1):
        band_copy(i).start()

    w_in = small_ref[0:8, :]
    w_out = small_ref[8:16, :]

    per_group = channels // GROUPS
    def group_of(axis):
        index = lax.broadcasted_iota(jnp.int32, (channels, channels), axis).astype(F32)
        return jnp.floor((index + 0.5) * (1.0 / per_group))
    same_group = jnp.where(group_of(0) == group_of(1), 1.0, 0.0).astype(BF16)

    step = step_ref[0]
    alpha_now = plan_at(step)
    alpha_prev = plan_at(step - STRIDE)
    scale_x = jnp.sqrt(alpha_prev) / jnp.sqrt(alpha_now)
    scale_noise = jnp.sqrt(1.0 - alpha_prev) - scale_x * jnp.sqrt(1.0 - alpha_now)

    lane = lax.broadcasted_iota(jnp.int32, (8, channels), 1)
    half_width = channels // 2
    harmonic_index = jnp.where(lane < half_width, lane, lane - half_width).astype(F32)
    frequency = jnp.exp(-math.log(10000.0) * harmonic_index / half_width)
    angle = step.astype(F32) * frequency
    harmonic = jnp.where(lane < half_width, jnp.cos(angle), jnp.sin(angle))

    loads[0].wait()
    pack_weights(raw_first, first_high, first_low, channels)
    loads[1].wait()
    embedded = silu(dot3(harmonic, raw_time[...]))[0:1, :]
    loads[2].wait()
    folded = jnp.concatenate(
        [dot3(w_out, raw_temporal[k], NT) for k in range(3)]
        + [jnp.zeros((8, channels), F32)],
        axis=0,
    )
    folded_high, folded_low = split(folded)
    w_out_high, w_out_low = split(
        jnp.concatenate([w_out, jnp.zeros((24, channels), F32)], axis=0)
    )
    loads[3].wait()
    pack_weights(raw_second, second_high, second_low, channels)

    border = jnp.zeros((width, 1024), BF16)
    for ref in (act_high, act_low):
        ref[0:width, :] = border
        ref[width + pixels :, :] = border
    rest_ref[0:width, :] = jnp.zeros((width, 256), F32)
    rest_ref[width + pixels :, :] = jnp.zeros((width, 256), F32)

    for i in range(n_band - 1):
        band_copy(i).wait()

    def from_band(j):
        found = pack_ref[...]
        for i in range(n_band - 1):
            found = jnp.where(lax.rem(band - i - 1 + n_band, n_band) == j, gathered[i], found)
        return found

    packs = [from_band(j) for j in range(n_band)]
    frame = jnp.concatenate([p[0:8] for p in packs], axis=1)
    entering = jnp.concatenate([p[8:16] for p in packs], axis=1)

    def norm_terms(ref):
        def add(i, sums):
            part = ref[pl.ds(pl.multiple_of(i * block, block), block), :]
            return (
                sums[0] + jnp.sum(part, axis=0, keepdims=True),
                sums[1] + jnp.sum(part * part, axis=0, keepdims=True),
            )

        zero = jnp.zeros((1, channels), F32)
        sums = lax.fori_loop(0, height // chunk, add, (zero, zero))
        row = lax.broadcasted_iota(jnp.int32, (16, channels), 0)
        stacked = jnp.zeros((16, channels), F32)
        for which, left in enumerate(sums):
            for part in range(3):
                piece = left.astype(BF16).astype(F32)
                left = left - piece
                stacked = jnp.where(row == which * 3 + part, piece, stacked)
        totals = dot(stacked.astype(BF16), same_group)
        members = float(pixels * per_group)
        center = (totals[0:1] + totals[1:2] + totals[2:3]) / members
        square = (totals[3:4] + totals[4:5] + totals[5:6]) / members
        return center, lax.rsqrt(square - center * center + EPSILON)

    column = lax.broadcasted_iota(jnp.int32, (width, channels), 0)

    def fill_act(ref, terms):
        center, factor = terms

        def one_row(i, carry):
            v = silu((ref[pl.ds(pl.multiple_of(i * width, width), width), :] - center) * factor)
            before = jnp.where(column == 0, 0.0, pltpu.roll(v, 1, 0))
            after = jnp.where(column == width - 1, 0.0, pltpu.roll(v, width - 1, 0))
            taps = (before, v, after)
            wide = jnp.concatenate(
                [t[:, 0:256] for t in taps]
                + [t[:, 256:channels] for t in taps]
                + [jnp.zeros((width, 1024 - 3 * channels), F32)],
                axis=1,
            )
            high, low = split(wide)
            place = pl.ds(pl.multiple_of((i + 1) * width, width), width)
            act_high[place, :] = high
            act_low[place, :] = low
            return carry

        lax.fori_loop(0, height, one_row, 0)

    def convolve(high_ref, low_ref, add):
        def product(start, n):
            place = pl.ds(pl.multiple_of(start, width), block)
            left = act_high[place, :]
            return (
                dot(left, high_ref[n])
                + dot(act_low[place, :], high_ref[n])
                + dot(left, low_ref[n])
            )

        def part(i, carry):
            base = i * block
            rest_ref[pl.ds(pl.multiple_of(base + width, width), block), :] = product(
                base + width, 3
            )
            total = product(base, 0) + product(base + width, 1)
            total = total + product(base + 2 * width, 2)
            place = pl.ds(pl.multiple_of(base, width), block)
            value_ref[place, 0:256] = total + add(place)[:, 0:256]
            return carry

        lax.fori_loop(0, height // chunk, part, 0)

        def end(i, carry):
            base = i * width
            total = add(pl.ds(pl.multiple_of(base, width), width))[:, 256:channels]
            for a in range(3):
                rows = pl.ds(pl.multiple_of(base + a * width, width), width)
                total = total + rest_ref[rows, a * rest : (a + 1) * rest]
            value_ref[pl.ds(pl.multiple_of(base, width), width), 256:channels] = total
            return carry

        lax.fori_loop(0, height, end, 0)

    def project(high, low, values):
        vh, vl = split(values)
        both = dot(jnp.concatenate([high, low], axis=0), vh, NT)
        return both[0:32] + both[32:64] + dot(high, vl, NT)

    def level_copy(i, source, target, to):
        return pltpu.make_async_remote_copy(
            src_ref=source,
            dst_ref=target,
            send_sem=level_send.at[i],
            recv_sem=level_recv.at[i],
            device_id={"level": to},
            device_id_type=MESH,
        )

    def run_block(frame):
        lifted_ref[...] = lax.dot_general(
            frame.T, w_in, NN, precision=lax.Precision.HIGHEST, preferred_element_type=F32
        )
        fill_act(lifted_ref, norm_terms(lifted_ref))
        convolve(first_high, first_low, lambda place: embedded)
        fill_act(value_ref, norm_terms(value_ref))
        convolve(second_high, second_low, lambda place: lifted_ref[place, :])
        return norm_terms(value_ref)

    center, factor = run_block(frame)
    hidden = value_ref[...]
    taps = project(folded_high, folded_low, silu((hidden - center) * factor))
    local = project(w_out_high, w_out_low, hidden)[0:8] + taps[8:16]
    send_frame[0:8, :] = scale_x * frame + scale_noise * local
    send_frame[8:16, :] = jnp.broadcast_to(scale_noise, (8, pixels))
    send_tap[...] = taps[0:8]
    frame_copy = level_copy(0, send_frame, recv_frame, level + 1)
    tap_copy = level_copy(1, send_tap, recv_tap, level + 2)
    pl.when(has_two_up)(lambda: tap_copy.start())
    pl.when(has_up)(lambda: frame_copy.start())
    pl.when(has_two_down)(lambda: tap_copy.wait_recv())
    pl.when(has_down)(lambda: frame_copy.wait_recv())
    moved = recv_frame[0:8, :] + recv_frame[8:16, :] * (recv_tap[...] + taps[16:24])
    frame = jnp.where(level == 0, entering, moved)
    pl.when(has_two_up)(lambda: tap_copy.wait_send())
    pl.when(has_up)(lambda: frame_copy.wait_send())

    center, factor = run_block(frame)
    hidden = value_ref[pl.ds(pl.multiple_of(band * held, width), held), :]
    taps = project(folded_high, folded_low, silu((hidden - center) * factor))
    send_last[0] = taps[0:8]
    send_last[1] = taps[16:24]
    up_copy = level_copy(2, send_last.at[0], recv_last.at[0], level + 1)
    down_copy = level_copy(3, send_last.at[1], recv_last.at[1], level - 1)
    pl.when(has_up)(lambda: up_copy.start())
    pl.when(has_down)(lambda: down_copy.start())
    local = project(w_out_high, w_out_low, hidden)[0:8] + taps[8:16]
    mine = frame[:, 0:held]
    for j in range(1, n_band):
        mine = jnp.where(band == j, frame[:, j * held : (j + 1) * held], mine)
    pl.when(has_down)(lambda: up_copy.wait_recv())
    pl.when(has_up)(lambda: down_copy.wait_recv())
    out_ref[...] = scale_x * mine + scale_noise * (local + recv_last[0] + recv_last[1])
    pl.when(has_up)(lambda: up_copy.wait_send())
    pl.when(has_down)(lambda: down_copy.wait_send())


def on_device(
    mesh_sizes, latents, timesteps, fresh, w_in, conv_first, conv_second, w_time, temporal, w_out
):
    n_level, n_band = mesh_sizes
    lat, band_rows, width = latents.shape[1:]
    channels = w_in.shape[1]
    height = band_rows * n_band
    pixels = height * width
    held = band_rows * width
    chunk = max(d for d in range(1, 11) if height % d == 0)

    def eight(rows):
        return jnp.pad(rows, ((0, 8 - lat), (0, 0)))

    pack = jnp.concatenate(
        [eight(latents[0].reshape(lat, held)), eight(fresh[0].reshape(lat, held))], axis=0
    )
    small = jnp.concatenate([eight(w_in), eight(w_out.T)], axis=0)

    vmem = pl.BlockSpec(memory_space=pltpu.VMEM)
    hbm = pl.BlockSpec(memory_space=pl.ANY)
    sem = pltpu.SemaphoreType.DMA
    result = pl.pallas_call(
        functools.partial(kernel, (n_level, n_band, channels, height, width, chunk)),
        out_shape=jax.ShapeDtypeStruct((8, held), F32),
        in_specs=[pl.BlockSpec(memory_space=pltpu.SMEM), vmem, vmem, hbm, hbm, hbm, hbm],
        out_specs=vmem,
        scratch_shapes=[
            pltpu.VMEM(conv_first.shape, F32),
            pltpu.VMEM(conv_second.shape, F32),
            pltpu.VMEM(w_time.shape, F32),
            pltpu.VMEM(temporal.shape, F32),
            *[pltpu.VMEM((4, 1024, 256), BF16)] * 4,
            *[pltpu.VMEM((pixels + 2 * width, 1024), BF16)] * 2,
            *[pltpu.VMEM((pixels, channels), F32)] * 2,
            pltpu.VMEM((pixels + 2 * width, 256), F32),
            pltpu.VMEM((max(n_band - 1, 1), 16, held), F32),
            *[pltpu.VMEM((16, pixels), F32)] * 2,
            *[pltpu.VMEM((8, pixels), F32)] * 2,
            *[pltpu.VMEM((2, 8, held), F32)] * 2,
            sem((4,)),
            sem((max(n_band - 1, 1),)),
            sem((max(n_band - 1, 1),)),
            sem((4,)),
            sem((4,)),
        ],
        compiler_params=pltpu.CompilerParams(
            collective_id=0, has_side_effects=True, vmem_limit_bytes=60 * 1024 * 1024
        ),
    )(timesteps, pack, small, conv_first, conv_second, w_time, temporal)
    return result[0:lat].reshape(1, lat, band_rows, width)


def solution(mesh):
    placed = (
        P("level", None, "band", None),
        P("level"),
        P(None, None, "band", None),
        P(),
        P(),
        P(),
        P(),
        P(),
        P(),
    )
    return jax.shard_map(
        functools.partial(on_device, (mesh.shape["level"], mesh.shape["band"])),
        mesh=mesh,
        in_specs=placed,
        out_specs=P("level", None, "band", None),
        check_vma=False,
    )
```

```python
import functools
import math

import jax
import jax.numpy as jnp
from jax import lax
from jax.experimental import pallas as pl
from jax.experimental.pallas import tpu as pltpu
from jax.sharding import PartitionSpec as P

GROUPS = 32
ITERS = 2
NSTEPS = 1000
STRIDE = 16
EPSILON = 1e-05

MESH = pl.DeviceIdType.MESH
F32 = jnp.float32
BF16 = jnp.bfloat16
NN = (((1,), (0,)), ((), ()))
NT = (((1,), (1,)), ((), ()))
TN = (((0,), (0,)), ((), ()))


def dot(a, b, dims=NN):
    return lax.dot_general(a, b, dims, preferred_element_type=F32)


def split(v):
    high = v.astype(BF16)
    return high, (v - high.astype(F32)).astype(BF16)


def dot3(a, b, dims=NN):
    ah, al = split(a)
    bh, bl = split(b)
    return dot(ah, bh, dims) + dot(al, bh, dims) + dot(ah, bl, dims)


def silu(v):
    half = 0.5 * v
    return half + half * jnp.tanh(half)


def plan_at(step):
    rows = -(-NSTEPS // 1024) * 8
    position = lax.broadcasted_iota(jnp.int32, (rows, 128), 0) * 128
    position = position + lax.broadcasted_iota(jnp.int32, (rows, 128), 1)
    root_beta = math.sqrt(0.00085) + position.astype(F32) / (NSTEPS - 1) * (
        math.sqrt(0.012) - math.sqrt(0.00085)
    )
    kept = jnp.where(position <= step, 1.0 - root_beta * root_beta, 1.0)
    for axis, length in ((0, rows), (1, 128)):
        shift = length // 2
        while shift:
            kept = kept * pltpu.roll(kept, shift, axis)
            shift //= 2
    return kept[0:1, 0:1]


def three_parts(v):
    parts = []
    for _ in range(3):
        piece = v.astype(BF16).astype(F32)
        parts.append(piece)
        v = v - piece
    return parts


def pack_weights(n, raw, high_ref, low_ref, channels):
    rest = channels - 256
    for ref in (high_ref, low_ref):
        ref[n, 3 * channels :, :] = jnp.zeros((1024 - 3 * channels, 256), BF16)
    for b in range(3):
        if n < 3:
            piece = raw[n, b, :, 0:256]
        else:
            piece = jnp.concatenate(
                [raw[a, b, :, 256:channels] for a in range(3)]
                + [jnp.zeros((channels, 256 - 3 * rest), F32)],
                axis=1,
            )
        high, low = split(piece)
        start = 768 + b * rest
        high_ref[n, b * 256 : (b + 1) * 256, :] = high[0:256]
        low_ref[n, b * 256 : (b + 1) * 256, :] = low[0:256]
        high_ref[n, start : start + rest, :] = high[256:channels]
        low_ref[n, start : start + rest, :] = low[256:channels]


def kernel(
    sizes,
    step_ref,
    latents_ref,
    fresh_ref,
    w_in_ref,
    w_out_ref,
    conv_first_hbm,
    conv_second_hbm,
    w_time_hbm,
    temporal_hbm,
    out_ref,
    raw_first,
    raw_second,
    raw_time,
    raw_temporal,
    first_high,
    first_low,
    second_high,
    second_low,
    act_high,
    act_low,
    lifted_ref,
    value_ref,
    rest_ref,
    pack_ref,
    gathered,
    send_frame,
    recv_frame,
    send_tap,
    recv_tap,
    send_last,
    recv_last,
    load_sem,
    band_send,
    band_recv,
    level_send,
    level_recv,
):
    n_level, n_band, channels, height, width, chunk = sizes
    rest = channels - 256
    pixels = height * width
    held = pixels // n_band
    block = chunk * width
    level = lax.axis_index("level")
    band = lax.axis_index("band")

    loads = [
        pltpu.make_async_copy(source, target, load_sem.at[i])
        for i, (source, target) in enumerate(
            (
                (conv_first_hbm, raw_first),
                (w_time_hbm, raw_time),
                (temporal_hbm, raw_temporal),
                (conv_second_hbm, raw_second),
            )
        )
    ]
    loads[0].start()
    loads[1].start()

    lat = latents_ref.shape[1]
    pack_ref[...] = jnp.zeros_like(pack_ref)
    for r in range(latents_ref.shape[0]):
        pack_ref[0:lat, r * width : (r + 1) * width] = latents_ref[r]
        pack_ref[8 : 8 + lat, r * width : (r + 1) * width] = fresh_ref[r]
    recv_frame[...] = jnp.zeros_like(recv_frame)
    recv_tap[...] = jnp.zeros_like(recv_tap)
    recv_last[...] = jnp.zeros_like(recv_last)

    has_up = level + 1 < n_level
    has_two_up = level + 2 < n_level
    has_down = level >= 1
    has_two_down = level >= 2

    barrier = pltpu.get_barrier_semaphore()
    peers = [lax.rem(band + i, n_band) for i in range(1, n_band)]

    def greet(who):
        pl.semaphore_signal(barrier, inc=1, device_id=who, device_id_type=MESH)

    for peer in peers:
        greet({"band": peer})
    pl.when(has_down)(lambda: greet({"level": level - 1}))
    pl.when(has_two_down)(lambda: greet({"level": level - 2}))
    pl.when(has_up)(lambda: greet({"level": level + 1}))
    expected = n_band - 1
    for there in (has_up, has_two_up, has_down):
        expected = expected + jnp.where(there, 1, 0)
    pl.semaphore_wait(barrier, expected)

    def band_copy(i):
        return pltpu.make_async_remote_copy(
            src_ref=pack_ref,
            dst_ref=gathered.at[i],
            send_sem=band_send.at[i],
            recv_sem=band_recv.at[i],
            device_id={"band": peers[i]},
            device_id_type=MESH,
        )

    for i in range(n_band - 1):
        band_copy(i).start()

    spare = jnp.zeros((8 - lat, channels), F32)
    w_in = jnp.concatenate([w_in_ref[...], spare], axis=0)
    w_out = jnp.concatenate([w_out_ref[...], spare], axis=0)

    per_group = channels // GROUPS
    def group_of(axis):
        index = lax.broadcasted_iota(jnp.int32, (channels, channels), axis).astype(F32)
        return jnp.floor((index + 0.5) * (1.0 / per_group))
    same_group = jnp.where(group_of(0) == group_of(1), 1.0, 0.0).astype(BF16)

    step = step_ref[0]
    alpha_now = plan_at(step)
    alpha_prev = plan_at(step - STRIDE)
    scale_x = jnp.sqrt(alpha_prev) / jnp.sqrt(alpha_now)
    scale_noise = jnp.sqrt(1.0 - alpha_prev) - scale_x * jnp.sqrt(1.0 - alpha_now)

    lane = lax.broadcasted_iota(jnp.int32, (8, channels), 1)
    half_width = channels // 2
    harmonic_index = jnp.where(lane < half_width, lane, lane - half_width).astype(F32)
    frequency = jnp.exp(-math.log(10000.0) * harmonic_index / half_width)
    angle = step.astype(F32) * frequency
    harmonic = jnp.where(lane < half_width, jnp.cos(angle), jnp.sin(angle))

    loads[0].wait()
    loads[2].start()
    loads[3].start()
    for n in range(4):
        pack_weights(n, raw_first, first_high, first_low, channels)
    loads[1].wait()
    embedded = silu(dot3(harmonic, raw_time[...]))[0:1, :]
    w_out_high, w_out_low = split(
        jnp.concatenate([w_out, jnp.zeros((24, channels), F32)], axis=0)
    )

    border = jnp.zeros((width, 1024), BF16)
    for ref in (act_high, act_low):
        ref[0:width, :] = border
        ref[width + pixels :, :] = border
    rest_ref[0:width, :] = jnp.zeros((width, 256), F32)
    rest_ref[width + pixels :, :] = jnp.zeros((width, 256), F32)

    for i in range(n_band - 1):
        band_copy(i).wait()

    def from_band(j):
        found = pack_ref[...]
        for i in range(n_band - 1):
            found = jnp.where(lax.rem(band - i - 1 + n_band, n_band) == j, gathered[i], found)
        return found

    packs = [from_band(j) for j in range(n_band)]
    frame = jnp.concatenate([p[0:8] for p in packs], axis=1)
    entering = jnp.concatenate([p[8:16] for p in packs], axis=1)

    def over_chunks(body):
        if height == chunk:
            body(0)
        else:
            lax.fori_loop(0, height // chunk, lambda i, c: (body(i * chunk), c)[1], 0)

    def image_row(i, count=1):
        start = i * width
        if not isinstance(start, int):
            start = pl.multiple_of(start, width)
        return pl.ds(start, count * width)

    def norm_terms(ref):
        def add(first):
            sums = []
            for i in range(chunk):
                part = ref[image_row(first + i), :].reshape(width // 8, 8, channels)
                sums.append((jnp.sum(part, axis=0), jnp.sum(part * part, axis=0)))
            while len(sums) > 1:
                pairs = [
                    (x[0] + y[0], x[1] + y[1]) for x, y in zip(sums[0::2], sums[1::2])
                ]
                sums = pairs + sums[2 * len(pairs) :]
            return sums[0]

        if height == chunk:
            sums = add(0)
        else:
            zero = jnp.zeros((8, channels), F32)

            def more(i, carry):
                part = add(i * chunk)
                return carry[0] + part[0], carry[1] + part[1]

            sums = lax.fori_loop(0, height // chunk, more, (zero, zero))
        row = lax.broadcasted_iota(jnp.int32, (16, channels), 0)
        stacked = jnp.zeros((16, channels), F32)
        for which, left in enumerate(sums):
            left = jnp.sum(left, axis=0, keepdims=True)
            for part, piece in enumerate(three_parts(left)):
                stacked = jnp.where(row == which * 3 + part, piece, stacked)
        totals = dot(stacked.astype(BF16), same_group)
        members = float(pixels * per_group)
        center = (totals[0:1] + totals[1:2] + totals[2:3]) / members
        square = (totals[3:4] + totals[4:5] + totals[5:6]) / members
        return center, lax.rsqrt(square - center * center + EPSILON)

    column = lax.broadcasted_iota(jnp.int32, (width, channels), 0)

    def fill_act(ref, terms):
        center, factor = terms

        def rows(first):
            for i in range(chunk):
                v = silu((ref[image_row(first + i), :] - center) * factor)
                before = jnp.where(column == 0, 0.0, pltpu.roll(v, 1, 0))
                after = jnp.where(column == width - 1, 0.0, pltpu.roll(v, width - 1, 0))
                taps = (before, v, after)
                wide = jnp.concatenate(
                    [t[:, 0:256] for t in taps]
                    + [t[:, 256:channels] for t in taps]
                    + [jnp.zeros((width, 1024 - 3 * channels), F32)],
                    axis=1,
                )
                high, low = split(wide)
                act_high[image_row(first + i + 1), :] = high
                act_low[image_row(first + i + 1), :] = low

        over_chunks(rows)

    half = chunk // 2 if chunk % 2 == 0 else chunk

    def convolve(high_ref, low_ref, add, beside=None):
        def depth(first, n):
            left = act_high[image_row(first, half), :]
            return (
                [left, act_low[image_row(first, half), :], left],
                [high_ref[n], high_ref[n], low_ref[n]],
            )

        def product(*terms):
            return dot(
                jnp.concatenate([x for left, _ in terms for x in left], axis=1),
                jnp.concatenate([x for _, right in terms for x in right], axis=0),
            )

        def rows(first):
            for i in range(0, chunk, half):
                at = first + i
                rest_ref[image_row(at + 1, half), :] = product(depth(at + 1, 3))
            for i in range(0, chunk, half):
                at = first + i
                total = product(depth(at, 0), depth(at + 1, 1), depth(at + 2, 2))
                place = image_row(at, half)
                value_ref[place, 0:256] = total + add(place)[:, 0:256]

        over_chunks(rows)
        if beside is not None:
            beside()

        def end(first):
            for i in range(chunk):
                place = image_row(first + i)
                total = add(place)[:, 256:channels]
                for a in range(3):
                    total = total + rest_ref[image_row(first + i + a), a * rest : (a + 1) * rest]
                value_ref[place, 256:channels] = total

        over_chunks(end)

    def project(high, low, values):
        vh, vl = split(values)
        both = dot(jnp.concatenate([high, low], axis=0), vh, NT)
        return both[0:32] + both[32:64] + dot(high, vl, NT)

    def level_copy(i, source, target, to):
        return pltpu.make_async_remote_copy(
            src_ref=source,
            dst_ref=target,
            send_sem=level_send.at[i],
            recv_sem=level_recv.at[i],
            device_id={"level": to},
            device_id_type=MESH,
        )

    wh, wm, wl = three_parts(w_in)
    w_in_parts = jnp.concatenate([wh, wm, wh, wm, wl, wh], axis=0).astype(BF16)

    def run_block(frame, beside=None):
        xh, xm, xl = three_parts(frame)
        left = jnp.concatenate([xh, xh, xm, xm, xh, xl], axis=0).T.astype(BF16)
        lifted_ref[...] = dot(left, w_in_parts)
        fill_act(lifted_ref, norm_terms(lifted_ref))
        convolve(first_high, first_low, lambda place: embedded, beside)
        fill_act(value_ref, norm_terms(value_ref))
        convolve(second_high, second_low, lambda place: lifted_ref[place, :])

    def prepare_later():
        for n in range(4):
            pack_weights(n, raw_second, second_high, second_low, channels)

    loads[2].wait()
    loads[3].wait()
    folded = jnp.concatenate(
        [dot3(w_out, raw_temporal[k], NT) for k in range(3)]
        + [jnp.zeros((8, channels), F32)],
        axis=0,
    )
    folded_high, folded_low = split(folded)
    run_block(frame, prepare_later)
    hidden = value_ref[...]
    straight = project(w_out_high, w_out_low, hidden)[0:8]
    center, factor = norm_terms(value_ref)
    taps = project(folded_high, folded_low, silu((hidden - center) * factor))
    send_frame[0:8, :] = scale_x * frame + scale_noise * (straight + taps[8:16])
    send_frame[8:16, :] = jnp.broadcast_to(scale_noise, (8, pixels))
    send_tap[...] = taps[0:8]
    frame_copy = level_copy(0, send_frame, recv_frame, level + 1)
    tap_copy = level_copy(1, send_tap, recv_tap, level + 2)
    pl.when(has_two_up)(lambda: tap_copy.start())
    pl.when(has_up)(lambda: frame_copy.start())
    pl.when(has_two_down)(lambda: tap_copy.wait_recv())
    pl.when(has_down)(lambda: frame_copy.wait_recv())
    moved = recv_frame[0:8, :] + recv_frame[8:16, :] * (recv_tap[...] + taps[16:24])
    frame = jnp.where(level == 0, entering, moved)
    pl.when(has_two_up)(lambda: tap_copy.wait_send())
    pl.when(has_up)(lambda: frame_copy.wait_send())

    run_block(frame)
    hidden = value_ref[pl.ds(pl.multiple_of(band * held, width), held), :]
    straight = project(w_out_high, w_out_low, hidden)[0:8]
    center, factor = norm_terms(value_ref)
    taps = project(folded_high, folded_low, silu((hidden - center) * factor))
    send_last[0] = taps[0:8]
    send_last[1] = taps[16:24]
    up_copy = level_copy(2, send_last.at[0], recv_last.at[0], level + 1)
    down_copy = level_copy(3, send_last.at[1], recv_last.at[1], level - 1)
    pl.when(has_up)(lambda: up_copy.start())
    pl.when(has_down)(lambda: down_copy.start())
    local = straight + taps[8:16]
    mine = frame[:, 0:held]
    for j in range(1, n_band):
        mine = jnp.where(band == j, frame[:, j * held : (j + 1) * held], mine)
    pl.when(has_down)(lambda: up_copy.wait_recv())
    pl.when(has_up)(lambda: down_copy.wait_recv())
    done = scale_x * mine + scale_noise * (local + recv_last[0] + recv_last[1])
    for r in range(out_ref.shape[0]):
        out_ref[r] = done[0:lat, r * width : (r + 1) * width]
    pl.when(has_up)(lambda: up_copy.wait_send())
    pl.when(has_down)(lambda: down_copy.wait_send())


def on_device(
    mesh_sizes, latents, timesteps, fresh, w_in, conv_first, conv_second, w_time, temporal, w_out
):
    n_level, n_band = mesh_sizes
    lat, band_rows, width = latents.shape[1:]
    channels = w_in.shape[1]
    height = band_rows * n_band
    pixels = height * width
    held = band_rows * width
    chunk = max(d for d in range(1, 11) if height % d == 0)

    vmem = pl.BlockSpec(memory_space=pltpu.VMEM)
    hbm = pl.BlockSpec(memory_space=pl.ANY)
    sem = pltpu.SemaphoreType.DMA
    result = pl.pallas_call(
        functools.partial(kernel, (n_level, n_band, channels, height, width, chunk)),
        out_shape=jax.ShapeDtypeStruct((band_rows, lat, width), F32),
        in_specs=[pl.BlockSpec(memory_space=pltpu.SMEM)] + [vmem] * 4 + [hbm] * 4,
        out_specs=vmem,
        scratch_shapes=[
            pltpu.VMEM(conv_first.shape, F32),
            pltpu.VMEM(conv_second.shape, F32),
            pltpu.VMEM(w_time.shape, F32),
            pltpu.VMEM(temporal.shape, F32),
            *[pltpu.VMEM((4, 1024, 256), BF16)] * 4,
            *[pltpu.VMEM((pixels + 2 * width, 1024), BF16)] * 2,
            *[pltpu.VMEM((pixels, channels), F32)] * 2,
            pltpu.VMEM((pixels + 2 * width, 256), F32),
            pltpu.VMEM((16, held), F32),
            pltpu.VMEM((max(n_band - 1, 1), 16, held), F32),
            *[pltpu.VMEM((16, pixels), F32)] * 2,
            *[pltpu.VMEM((8, pixels), F32)] * 2,
            *[pltpu.VMEM((2, 8, held), F32)] * 2,
            sem((4,)),
            sem((max(n_band - 1, 1),)),
            sem((max(n_band - 1, 1),)),
            sem((4,)),
            sem((4,)),
        ],
        compiler_params=pltpu.CompilerParams(
            collective_id=0, has_side_effects=True, vmem_limit_bytes=60 * 1024 * 1024
        ),
    )(
        timesteps,
        latents[0].transpose(1, 0, 2),
        fresh[0].transpose(1, 0, 2),
        w_in,
        w_out.T,
        conv_first,
        conv_second,
        w_time,
        temporal,
    )
    return result.transpose(1, 0, 2)[None]


def solution(mesh):
    placed = (
        P("level", None, "band", None),
        P("level"),
        P(None, None, "band", None),
        P(),
        P(),
        P(),
        P(),
        P(),
        P(),
    )
    return jax.shard_map(
        functools.partial(on_device, (mesh.shape["level"], mesh.shape["band"])),
        mesh=mesh,
        in_specs=placed,
        out_specs=P("level", None, "band", None),
        check_vma=False,
    )
```

```python
import functools
import math

import jax
import jax.numpy as jnp
from jax import lax
from jax.experimental import pallas as pl
from jax.experimental.pallas import tpu as pltpu
from jax.sharding import PartitionSpec as P

GROUPS = 32
ITERS = 2
NSTEPS = 1000
STRIDE = 16
EPSILON = 1e-05

MESH = pl.DeviceIdType.MESH
F32 = jnp.float32
BF16 = jnp.bfloat16
NN = (((1,), (0,)), ((), ()))
NT = (((1,), (1,)), ((), ()))
TN = (((0,), (0,)), ((), ()))


def dot(a, b, dims=NN):
    return lax.dot_general(a, b, dims, preferred_element_type=F32)


def split(v):
    high = v.astype(BF16)
    return high, (v - high.astype(F32)).astype(BF16)


def dot3(a, b, dims=NN):
    ah, al = split(a)
    bh, bl = split(b)
    return dot(ah, bh, dims) + dot(al, bh, dims) + dot(ah, bl, dims)


def silu(v):
    half = 0.5 * v
    return half + half * jnp.tanh(half)


def plan_at(step):
    rows = -(-NSTEPS // 1024) * 8
    position = lax.broadcasted_iota(jnp.int32, (rows, 128), 0) * 128
    position = position + lax.broadcasted_iota(jnp.int32, (rows, 128), 1)
    root_beta = math.sqrt(0.00085) + position.astype(F32) / (NSTEPS - 1) * (
        math.sqrt(0.012) - math.sqrt(0.00085)
    )
    kept = jnp.where(position <= step, 1.0 - root_beta * root_beta, 1.0)
    for axis, length in ((0, rows), (1, 128)):
        shift = length // 2
        while shift:
            kept = kept * pltpu.roll(kept, shift, axis)
            shift //= 2
    return kept[0:1, 0:1]


def three_parts(v):
    parts = []
    for _ in range(3):
        piece = v.astype(BF16).astype(F32)
        parts.append(piece)
        v = v - piece
    return parts


def pack_weights(n, raw, high_ref, low_ref, channels):
    rest = channels - 256
    for ref in (high_ref, low_ref):
        ref[n, 3 * channels :, :] = jnp.zeros((1024 - 3 * channels, 256), BF16)
    for b in range(3):
        if n < 3:
            piece = raw[n, b, :, 0:256]
        else:
            piece = jnp.concatenate(
                [raw[a, b, :, 256:channels] for a in range(3)]
                + [jnp.zeros((channels, 256 - 3 * rest), F32)],
                axis=1,
            )
        high, low = split(piece)
        start = 768 + b * rest
        high_ref[n, b * 256 : (b + 1) * 256, :] = high[0:256]
        low_ref[n, b * 256 : (b + 1) * 256, :] = low[0:256]
        high_ref[n, start : start + rest, :] = high[256:channels]
        low_ref[n, start : start + rest, :] = low[256:channels]


def kernel(
    sizes,
    step_hbm,
    latents_hbm,
    fresh_hbm,
    w_in_hbm,
    w_out_hbm,
    conv_first_hbm,
    conv_second_hbm,
    w_time_hbm,
    temporal_hbm,
    out_ref,
    step_ref,
    latents_ref,
    fresh_ref,
    w_in_ref,
    w_out_ref,
    raw_first,
    raw_second,
    raw_time,
    raw_temporal,
    first_high,
    first_low,
    second_high,
    second_low,
    act_high,
    act_low,
    lifted_ref,
    first_ref,
    hidden_ref,
    rest_ref,
    pack_ref,
    gathered,
    stat_mine,
    stat_theirs,
    send_frame,
    recv_frame,
    send_tap,
    recv_tap,
    send_back,
    recv_back,
    send_last,
    recv_last,
    load_sem,
    band_send,
    band_recv,
    stat_send,
    stat_recv,
    frame_send,
    frame_recv,
    tap_send,
    tap_recv,
    back_send,
    back_recv,
    last_send,
    last_recv,
):
    n_level, n_band, channels, height, width, n_first = sizes
    rest = channels - 256
    pixels = height * width
    own = height // n_band
    held = own * width
    level = lax.axis_index("level")
    band = lax.axis_index("band")
    start = jnp.where(band == n_band - 1, height - n_first, band * own - 1)
    start = jnp.where(band == 0, 0, start)
    inset = band * own - start

    loads = [
        pltpu.make_async_copy(source, target, load_sem.at[i])
        for i, (source, target) in enumerate(
            (
                (latents_hbm, latents_ref),
                (fresh_hbm, fresh_ref),
                (step_hbm, step_ref),
                (w_in_hbm, w_in_ref),
                (w_out_hbm, w_out_ref),
                (conv_first_hbm, raw_first),
                (w_time_hbm, raw_time),
                (temporal_hbm, raw_temporal),
                (conv_second_hbm, raw_second),
            )
        )
    ]
    for load in loads[:7]:
        load.start()

    recv_frame[...] = jnp.zeros_like(recv_frame)
    recv_tap[...] = jnp.zeros_like(recv_tap)
    recv_last[...] = jnp.zeros_like(recv_last)

    has_up = level + 1 < n_level
    has_two_up = level + 2 < n_level
    has_down = level >= 1
    has_two_down = level >= 2

    barrier = pltpu.get_barrier_semaphore()
    others = [lax.rem(band + i, n_band) for i in range(n_band)]
    peers = others[1:]

    def greet(*who):
        for one in who:
            pl.semaphore_signal(barrier, inc=1, device_id=one, device_id_type=MESH)

    greet(*[{"band": peer} for peer in peers])
    pl.when(has_down)(lambda: greet(*[{"level": level - 1, "band": o} for o in others]))
    pl.when(has_two_down)(lambda: greet(*[{"level": level - 2, "band": o} for o in others]))
    pl.when(has_up)(lambda: greet({"level": level + 1}))

    lat = latents_ref.shape[1]
    pack_ref[...] = jnp.zeros_like(pack_ref)
    loads[0].wait()
    loads[1].wait()
    for r in range(own):
        pack_ref[0:lat, r * width : (r + 1) * width] = latents_ref[r]
        pack_ref[8 : 8 + lat, r * width : (r + 1) * width] = fresh_ref[r]

    expected = n_band - 1
    for there, count in ((has_up, n_band), (has_two_up, n_band), (has_down, 1)):
        expected = expected + jnp.where(there, count, 0)
    pl.semaphore_wait(barrier, expected)

    def remote(source, target, sent, arrived, to):
        return pltpu.make_async_remote_copy(
            src_ref=source,
            dst_ref=target,
            send_sem=sent,
            recv_sem=arrived,
            device_id=to,
            device_id_type=MESH,
        )

    band_copies = [
        remote(pack_ref, gathered.at[i], band_send.at[i], band_recv.at[i], {"band": peers[i]})
        for i in range(n_band - 1)
    ]
    for copy in band_copies:
        copy.start()

    def by_band(slots):
        found = []
        for j in range(n_band):
            block = slots[0]
            for i in range(1, n_band):
                block = jnp.where(lax.rem(band - i + n_band, n_band) == j, slots[i], block)
            found.append(block)
        return found

    per_group = channels // GROUPS

    def group_of(axis):
        index = lax.broadcasted_iota(jnp.int32, (channels, channels), axis).astype(F32)
        return jnp.floor((index + 0.5) * (1.0 / per_group))

    same_group = jnp.where(group_of(0) == group_of(1), 1.0, 0.0).astype(BF16)

    for load in loads[2:5]:
        load.wait()
    spare = jnp.zeros((8 - lat, channels), F32)
    w_in = jnp.concatenate([w_in_ref[...], spare], axis=0)
    w_out = jnp.concatenate([w_out_ref[...], spare], axis=0)
    wh, wm, wl = three_parts(w_in)
    w_in_parts = jnp.concatenate([wh, wm, wh, wm, wl, wh], axis=0).astype(BF16)

    step = step_ref[0]
    alpha_now = plan_at(step)
    alpha_prev = plan_at(step - STRIDE)
    scale_x = jnp.sqrt(alpha_prev) / jnp.sqrt(alpha_now)
    scale_noise = jnp.sqrt(1.0 - alpha_prev) - scale_x * jnp.sqrt(1.0 - alpha_now)

    lane = lax.broadcasted_iota(jnp.int32, (8, channels), 1)
    half_width = channels // 2
    harmonic_index = jnp.where(lane < half_width, lane, lane - half_width).astype(F32)
    frequency = jnp.exp(-math.log(10000.0) * harmonic_index / half_width)
    angle = step.astype(F32) * frequency
    harmonic = jnp.where(lane < half_width, jnp.cos(angle), jnp.sin(angle))

    lifted_ref[0:width, :] = jnp.zeros((width, channels), F32)
    lifted_ref[width + pixels :, :] = jnp.zeros((width, channels), F32)
    first_ref[0:width, :] = jnp.zeros((width, channels), F32)
    first_ref[(n_first + 1) * width :, :] = jnp.zeros((width, channels), F32)
    rest_ref[...] = jnp.zeros_like(rest_ref)

    loads[5].wait()
    loads[7].start()
    loads[8].start()
    for n in range(4):
        pack_weights(n, raw_first, first_high, first_low, channels)
    loads[6].wait()
    embedded = silu(dot3(harmonic, raw_time[...]))[0:1, :]
    w_out_high, w_out_low = split(
        jnp.concatenate([w_out, jnp.zeros((24, channels), F32)], axis=0)
    )

    for copy in band_copies:
        copy.wait()

    packs = by_band([pack_ref[...]] + [gathered[i] for i in range(n_band - 1)])
    frame = jnp.concatenate([p[0:8] for p in packs], axis=1)
    entering = jnp.concatenate([p[8:16] for p in packs], axis=1)

    def image_row(i, count=1):
        at = i * width
        if not isinstance(at, int):
            at = pl.multiple_of(at, width)
        return pl.ds(at, count * width)

    def local_sums(ref, first, count):
        sums = []
        for i in range(count):
            part = ref[image_row(first + i), :].reshape(width // 8, 8, channels)
            sums.append((jnp.sum(part, axis=0), jnp.sum(part * part, axis=0)))
        while len(sums) > 1:
            pairs = [(x[0] + y[0], x[1] + y[1]) for x, y in zip(sums[0::2], sums[1::2])]
            sums = pairs + sums[2 * len(pairs) :]
        return [jnp.sum(x, axis=0, keepdims=True) for x in sums[0]]

    def norm_terms(sums):
        row = lax.broadcasted_iota(jnp.int32, (16, channels), 0)
        stacked = jnp.zeros((16, channels), F32)
        for which, left in enumerate(sums):
            for part, piece in enumerate(three_parts(left)):
                stacked = jnp.where(row == which * 3 + part, piece, stacked)
        totals = dot(stacked.astype(BF16), same_group)
        members = float(pixels * per_group)
        center = (totals[0:1] + totals[1:2] + totals[2:3]) / members
        square = (totals[3:4] + totals[4:5] + totals[5:6]) / members
        return center, lax.rsqrt(square - center * center + EPSILON)

    def shared_terms(turn, ref, first):
        sums = local_sums(ref, first, own)
        stat_mine[turn, 0:1, :] = sums[0]
        stat_mine[turn, 1:2, :] = sums[1]
        stat_mine[turn, 2:8, :] = jnp.zeros((6, channels), F32)
        copies = [
            remote(
                stat_mine.at[turn],
                stat_theirs.at[turn, i],
                stat_send.at[turn, i],
                stat_recv.at[turn, i],
                {"band": peers[i]},
            )
            for i in range(n_band - 1)
        ]
        for copy in copies:
            copy.start()
        for copy in copies:
            copy.wait()
        for i in range(n_band - 1):
            sums = [x + stat_theirs[turn, i, w : w + 1, :] for w, x in enumerate(sums)]
        return norm_terms(sums)

    column = lax.broadcasted_iota(jnp.int32, (width, channels), 0)

    def fill_act(ref, first, top, count, terms):
        center, factor = terms
        for i in range(count):
            v = silu((ref[image_row(first + i), :] - center) * factor)
            if i == 0:
                v = jnp.where(top < 0, 0.0, v)
            if i == count - 1:
                v = jnp.where(top + i >= height, 0.0, v)
            before = jnp.where(column == 0, 0.0, pltpu.roll(v, 1, 0))
            after = jnp.where(column == width - 1, 0.0, pltpu.roll(v, width - 1, 0))
            taps = (before, v, after)
            wide = jnp.concatenate(
                [t[:, 0:256] for t in taps]
                + [t[:, 256:channels] for t in taps]
                + [jnp.zeros((width, 1024 - 3 * channels), F32)],
                axis=1,
            )
            high, low = split(wide)
            act_high[image_row(i), :] = high
            act_low[image_row(i), :] = low

    def convolve(high_ref, low_ref, count, add, out, out_first, beside=None):
        part = max(d for d in range(1, 7) if count % d == 0)

        def depth(first, n, size):
            left = act_high[image_row(first, size), :]
            return (
                [left, act_low[image_row(first, size), :], left],
                [high_ref[n], high_ref[n], low_ref[n]],
            )

        def product(*terms):
            return dot(
                jnp.concatenate([x for left, _ in terms for x in left], axis=1),
                jnp.concatenate([x for _, right in terms for x in right], axis=0),
            )

        filled = count + 2
        share = max(d for d in range(1, 8) if filled % d == 0)
        for i in range(0, filled, share):
            rest_ref[image_row(i, share), :] = product(depth(i, 3, share))
        for i in range(0, count, part):
            total = product(depth(i, 0, part), depth(i + 1, 1, part), depth(i + 2, 2, part))
            out[image_row(out_first + i, part), 0:256] = total + add(i, part)[:, 0:256]
        if beside is not None:
            beside()
        for i in range(count):
            total = add(i, 1)[:, 256:channels]
            for a in range(3):
                total = total + rest_ref[image_row(i + a), a * rest : (a + 1) * rest]
            out[image_row(out_first + i), 256:channels] = total

    def project(high, low, values):
        vh, vl = split(values)
        both = dot(jnp.concatenate([high, low], axis=0), vh, NT)
        return both[0:32] + both[32:64] + dot(high, vl, NT)

    def run_block(iteration, frame, beside=None):
        xh, xm, xl = three_parts(frame)
        left = jnp.concatenate([xh, xh, xm, xm, xh, xl], axis=0).T.astype(BF16)
        lifted_ref[width : width + pixels, :] = dot(left, w_in_parts)
        terms = norm_terms(local_sums(lifted_ref, 1, height))
        fill_act(lifted_ref, start, start - 1, n_first + 2, terms)
        convolve(
            first_high, first_low, n_first, lambda i, size: embedded, first_ref, 1, beside
        )
        terms = shared_terms(2 * iteration, first_ref, 1 + inset)
        fill_act(first_ref, inset, band * own - 1, own + 2, terms)
        convolve(
            second_high,
            second_low,
            own,
            lambda i, size: lifted_ref[image_row(band * own + 1 + i, size), :],
            hidden_ref,
            0,
        )
        hidden = hidden_ref[...]
        straight = project(w_out_high, w_out_low, hidden)[0:8]
        center, factor = shared_terms(2 * iteration + 1, hidden_ref, 0)
        taps = project(folded_high, folded_low, silu((hidden - center) * factor))
        return straight + taps[8:16], taps

    def mine_of(frame):
        mine = frame[:, 0:held]
        for j in range(1, n_band):
            mine = jnp.where(band == j, frame[:, j * held : (j + 1) * held], mine)
        return mine

    def prepare_later():
        for n in range(4):
            pack_weights(n, raw_second, second_high, second_low, channels)

    loads[7].wait()
    loads[8].wait()
    folded = jnp.concatenate(
        [dot3(w_out, raw_temporal[k], NT) for k in range(3)]
        + [jnp.zeros((8, channels), F32)],
        axis=0,
    )
    folded_high, folded_low = split(folded)

    local, taps = run_block(0, frame, prepare_later)
    send_tap[...] = taps[0:8]
    send_back[...] = taps[16:24]
    tap_copies = [
        remote(
            send_tap, recv_tap.at[i], tap_send.at[i], tap_recv.at[i], {"level": level + 2, "band": o}
        )
        for i, o in enumerate(others)
    ]
    frame_copies = [
        remote(
            send_frame,
            recv_frame.at[i],
            frame_send.at[i],
            frame_recv.at[i],
            {"level": level + 1, "band": o},
        )
        for i, o in enumerate(others)
    ]
    back_copies = [
        remote(send_back, recv_back.at[i], back_send.at[i], back_recv.at[i], {"band": peers[i]})
        for i in range(n_band - 1)
    ]

    def each(action, copies):
        for copy in copies:
            getattr(copy, action)()

    pl.when(has_two_up)(lambda: each("start", tap_copies))
    send_frame[0:4, :] = (scale_x * mine_of(frame) + scale_noise * local)[0:4]
    send_frame[4:8, :] = jnp.broadcast_to(scale_noise, (4, held))
    pl.when(has_up)(lambda: each("start", frame_copies))
    each("start", back_copies)
    each("wait", back_copies)
    pl.when(has_two_down)(lambda: each("wait_recv", tap_copies))
    pl.when(has_down)(lambda: each("wait_recv", frame_copies))
    slots = [taps[16:24]] + [recv_back[i] for i in range(n_band - 1)]
    moved = []
    for i in range(n_band):
        turned = recv_frame[i][4:8] * (recv_tap[i] + slots[i])[0:4]
        moved.append(recv_frame[i][0:4] + turned)
    moved = jnp.concatenate(by_band(moved), axis=1)
    moved = jnp.concatenate([moved, jnp.zeros((4, pixels), F32)], axis=0)
    frame = jnp.where(level == 0, entering, moved)
    pl.when(has_two_up)(lambda: each("wait_send", tap_copies))
    pl.when(has_up)(lambda: each("wait_send", frame_copies))

    local, taps = run_block(1, frame)
    send_last[0] = taps[0:8]
    send_last[1] = taps[16:24]
    up_copy, down_copy = (
        remote(
            send_last.at[i], recv_last.at[i], last_send.at[i], last_recv.at[i], {"level": to}
        )
        for i, to in enumerate((level + 1, level - 1))
    )
    pl.when(has_up)(lambda: up_copy.start())
    pl.when(has_down)(lambda: down_copy.start())
    done = scale_x * mine_of(frame) + scale_noise * local
    pl.when(has_down)(lambda: up_copy.wait_recv())
    pl.when(has_up)(lambda: down_copy.wait_recv())
    done = done + scale_noise * (recv_last[0] + recv_last[1])
    for r in range(own):
        out_ref[r] = done[0:lat, r * width : (r + 1) * width]
    pl.when(has_up)(lambda: up_copy.wait_send())
    pl.when(has_down)(lambda: down_copy.wait_send())


def on_device(
    mesh_sizes, latents, timesteps, fresh, w_in, conv_first, conv_second, w_time, temporal, w_out
):
    n_level, n_band = mesh_sizes
    lat, band_rows, width = latents.shape[1:]
    channels = w_in.shape[1]
    height = band_rows * n_band
    pixels = height * width
    held = band_rows * width
    n_first = min(height, band_rows + min(n_band - 1, 2))
    others = max(n_band - 1, 1)

    vmem = pl.BlockSpec(memory_space=pltpu.VMEM)
    hbm = pl.BlockSpec(memory_space=pl.ANY)
    sem = pltpu.SemaphoreType.DMA
    result = pl.pallas_call(
        functools.partial(kernel, (n_level, n_band, channels, height, width, n_first)),
        out_shape=jax.ShapeDtypeStruct((band_rows, lat, width), F32),
        in_specs=[hbm] * 9,
        out_specs=vmem,
        scratch_shapes=[
            pltpu.SMEM((1,), jnp.int32),
            *[pltpu.VMEM((band_rows, lat, width), F32)] * 2,
            *[pltpu.VMEM((lat, channels), F32)] * 2,
            pltpu.VMEM(conv_first.shape, F32),
            pltpu.VMEM(conv_second.shape, F32),
            pltpu.VMEM(w_time.shape, F32),
            pltpu.VMEM(temporal.shape, F32),
            *[pltpu.VMEM((4, 1024, 256), BF16)] * 4,
            *[pltpu.VMEM(((n_first + 2) * width, 1024), BF16)] * 2,
            pltpu.VMEM(((height + 2) * width, channels), F32),
            pltpu.VMEM(((n_first + 2) * width, channels), F32),
            pltpu.VMEM((held, channels), F32),
            pltpu.VMEM(((n_first + 2) * width, 256), F32),
            pltpu.VMEM((16, held), F32),
            pltpu.VMEM((others, 16, held), F32),
            pltpu.VMEM((2 * ITERS, 8, channels), F32),
            pltpu.VMEM((2 * ITERS, others, 8, channels), F32),
            *[pltpu.VMEM((8, held), F32), pltpu.VMEM((n_band, 8, held), F32)] * 2,
            *[pltpu.VMEM((8, held), F32), pltpu.VMEM((others, 8, held), F32)],
            *[pltpu.VMEM((2, 8, held), F32)] * 2,
            sem((9,)),
            *[sem((others,))] * 2,
            *[sem((2 * ITERS, others))] * 2,
            *[sem((n_band,))] * 4,
            *[sem((others,))] * 2,
            *[sem((2,))] * 2,
        ],
        compiler_params=pltpu.CompilerParams(
            collective_id=0, has_side_effects=True, vmem_limit_bytes=60 * 1024 * 1024
        ),
    )(
        timesteps,
        latents[0].transpose(1, 0, 2),
        fresh[0].transpose(1, 0, 2),
        w_in,
        w_out.T,
        conv_first,
        conv_second,
        w_time,
        temporal,
    )
    return result.transpose(1, 0, 2)[None]


def solution(mesh):
    placed = (
        P("level", None, "band", None),
        P("level"),
        P(None, None, "band", None),
        P(),
        P(),
        P(),
        P(),
        P(),
        P(),
    )
    return jax.shard_map(
        functools.partial(on_device, (mesh.shape["level"], mesh.shape["band"])),
        mesh=mesh,
        in_specs=placed,
        out_specs=P("level", None, "band", None),
        check_vma=False,
    )
```

```python
import functools
import math

import jax
import jax.numpy as jnp
from jax import lax
from jax.experimental import pallas as pl
from jax.experimental.pallas import tpu as pltpu
from jax.sharding import PartitionSpec as P

GROUPS = 32
ITERS = 2
NSTEPS = 1000
STRIDE = 16
EPSILON = 1e-05

MESH = pl.DeviceIdType.MESH
F32 = jnp.float32
BF16 = jnp.bfloat16
NN = (((1,), (0,)), ((), ()))
NT = (((1,), (1,)), ((), ()))
TN = (((0,), (0,)), ((), ()))


def dot(a, b, dims=NN):
    return lax.dot_general(a, b, dims, preferred_element_type=F32)


def split(v):
    high = v.astype(BF16)
    return high, (v - high.astype(F32)).astype(BF16)


def dot3(a, b, dims=NN):
    ah, al = split(a)
    bh, bl = split(b)
    return dot(ah, bh, dims) + dot(al, bh, dims) + dot(ah, bl, dims)


def silu(v):
    half = 0.5 * v
    return half + half * jnp.tanh(half)


def plan_at(step):
    rows = -(-NSTEPS // 1024) * 8
    position = lax.broadcasted_iota(jnp.int32, (rows, 128), 0) * 128
    position = position + lax.broadcasted_iota(jnp.int32, (rows, 128), 1)
    root_beta = math.sqrt(0.00085) + position.astype(F32) / (NSTEPS - 1) * (
        math.sqrt(0.012) - math.sqrt(0.00085)
    )
    kept = jnp.where(position <= step, 1.0 - root_beta * root_beta, 1.0)
    for axis, length in ((0, rows), (1, 128)):
        shift = length // 2
        while shift:
            kept = kept * pltpu.roll(kept, shift, axis)
            shift //= 2
    return kept[0:1, 0:1]


def three_parts(v):
    parts = []
    for _ in range(3):
        piece = v.astype(BF16).astype(F32)
        parts.append(piece)
        v = v - piece
    return parts


def pack_weights(n, raw, high_ref, low_ref, channels):
    rest = channels - 256
    for ref in (high_ref, low_ref):
        ref[n, 3 * channels :, :] = jnp.zeros((1024 - 3 * channels, 256), BF16)
    for b in range(3):
        if n < 3:
            piece = raw[n, b, :, 0:256]
        else:
            piece = jnp.concatenate(
                [raw[a, b, :, 256:channels] for a in range(3)]
                + [jnp.zeros((channels, 256 - 3 * rest), F32)],
                axis=1,
            )
        high, low = split(piece)
        start = 768 + b * rest
        high_ref[n, b * 256 : (b + 1) * 256, :] = high[0:256]
        low_ref[n, b * 256 : (b + 1) * 256, :] = low[0:256]
        high_ref[n, start : start + rest, :] = high[256:channels]
        low_ref[n, start : start + rest, :] = low[256:channels]


def kernel(
    sizes,
    step_hbm,
    latents_hbm,
    fresh_hbm,
    w_in_hbm,
    w_out_hbm,
    conv_first_hbm,
    conv_second_hbm,
    w_time_hbm,
    temporal_hbm,
    out_ref,
    late_ref,
    step_ref,
    latents_ref,
    fresh_ref,
    w_in_ref,
    w_out_ref,
    raw_first,
    raw_second,
    raw_time,
    raw_temporal,
    first_high,
    first_low,
    second_high,
    second_low,
    act_high,
    act_low,
    lifted_ref,
    value_ref,
    rest_ref,
    pack_ref,
    gathered,
    send_frame,
    recv_frame,
    send_tap,
    recv_tap,
    send_last,
    recv_last,
    load_sem,
    band_send,
    band_recv,
    level_send,
    level_recv,
):
    n_level, n_band, channels, height, width, chunk = sizes
    rest = channels - 256
    pixels = height * width
    held = pixels // n_band
    block = chunk * width
    level = lax.axis_index("level")
    band = lax.axis_index("band")

    loads = [
        pltpu.make_async_copy(source, target, load_sem.at[i])
        for i, (source, target) in enumerate(
            (
                (latents_hbm, latents_ref),
                (fresh_hbm, fresh_ref),
                (step_hbm, step_ref),
                (w_in_hbm, w_in_ref),
                (w_out_hbm, w_out_ref),
                (conv_first_hbm, raw_first),
                (w_time_hbm, raw_time),
                (temporal_hbm, raw_temporal),
                (conv_second_hbm, raw_second),
            )
        )
    ]
    for load in loads[:7]:
        load.start()

    recv_frame[...] = jnp.zeros_like(recv_frame)
    recv_tap[...] = jnp.zeros_like(recv_tap)
    recv_last[...] = jnp.zeros_like(recv_last)

    has_up = level + 1 < n_level
    has_two_up = level + 2 < n_level
    has_down = level >= 1
    has_two_down = level >= 2

    barrier = pltpu.get_barrier_semaphore()
    peers = [lax.rem(band + i, n_band) for i in range(1, n_band)]

    def greet(who):
        pl.semaphore_signal(barrier, inc=1, device_id=who, device_id_type=MESH)

    for peer in peers:
        greet({"band": peer})
    pl.when(has_down)(lambda: greet({"level": level - 1}))
    pl.when(has_two_down)(lambda: greet({"level": level - 2}))
    pl.when(has_up)(lambda: greet({"level": level + 1}))
    lat = latents_ref.shape[1]
    pack_ref[...] = jnp.zeros_like(pack_ref)
    loads[0].wait()
    loads[1].wait()
    for r in range(latents_ref.shape[0]):
        pack_ref[0:lat, r * width : (r + 1) * width] = latents_ref[r]
        pack_ref[8 : 8 + lat, r * width : (r + 1) * width] = fresh_ref[r]
    loads[7].start()
    loads[8].start()

    expected = n_band - 1
    for there in (has_up, has_two_up, has_down):
        expected = expected + jnp.where(there, 1, 0)
    pl.semaphore_wait(barrier, expected)

    def band_copy(i):
        return pltpu.make_async_remote_copy(
            src_ref=pack_ref,
            dst_ref=gathered.at[i],
            send_sem=band_send.at[i],
            recv_sem=band_recv.at[i],
            device_id={"band": peers[i]},
            device_id_type=MESH,
        )

    for i in range(n_band - 1):
        band_copy(i).start()

    for load in loads[2:5]:
        load.wait()
    spare = jnp.zeros((8 - lat, channels), F32)
    w_in = jnp.concatenate([w_in_ref[...], spare], axis=0)
    w_out = jnp.concatenate([w_out_ref[...], spare], axis=0)

    per_group = channels // GROUPS
    def group_of(axis):
        index = lax.broadcasted_iota(jnp.int32, (channels, channels), axis).astype(F32)
        return jnp.floor((index + 0.5) * (1.0 / per_group))
    same_group = jnp.where(group_of(0) == group_of(1), 1.0, 0.0).astype(BF16)

    step = step_ref[0]
    alpha_now = plan_at(step)
    alpha_prev = plan_at(step - STRIDE)
    scale_x = jnp.sqrt(alpha_prev) / jnp.sqrt(alpha_now)
    scale_noise = jnp.sqrt(1.0 - alpha_prev) - scale_x * jnp.sqrt(1.0 - alpha_now)

    lane = lax.broadcasted_iota(jnp.int32, (8, channels), 1)
    half_width = channels // 2
    harmonic_index = jnp.where(lane < half_width, lane, lane - half_width).astype(F32)
    frequency = jnp.exp(-math.log(10000.0) * harmonic_index / half_width)
    angle = step.astype(F32) * frequency
    harmonic = jnp.where(lane < half_width, jnp.cos(angle), jnp.sin(angle))

    loads[5].wait()
    for n in range(4):
        pack_weights(n, raw_first, first_high, first_low, channels)
    loads[6].wait()
    embedded = silu(dot3(harmonic, raw_time[...]))[0:1, :]
    w_out_high, w_out_low = split(
        jnp.concatenate([w_out, jnp.zeros((24, channels), F32)], axis=0)
    )

    loads[7].wait()
    folded = jnp.concatenate(
        [dot3(w_out, raw_temporal[k], NT) for k in range(3)]
        + [jnp.zeros((8, channels), F32)],
        axis=0,
    )
    folded_high, folded_low = split(folded)
    loads[8].wait()
    for n in range(4):
        pack_weights(n, raw_second, second_high, second_low, channels)

    border = jnp.zeros((width, 1024), BF16)
    for ref in (act_high, act_low):
        ref[0:width, :] = border
        ref[width + pixels :, :] = border
    rest_ref[0:width, :] = jnp.zeros((width, 256), F32)
    rest_ref[width + pixels :, :] = jnp.zeros((width, 256), F32)

    for i in range(n_band - 1):
        band_copy(i).wait()

    def from_band(j):
        found = pack_ref[...]
        for i in range(n_band - 1):
            found = jnp.where(lax.rem(band - i - 1 + n_band, n_band) == j, gathered[i], found)
        return found

    packs = [from_band(j) for j in range(n_band)]
    frame = jnp.concatenate([p[0:8] for p in packs], axis=1)
    entering = jnp.concatenate([p[8:16] for p in packs], axis=1)

    def over_chunks(body):
        if height == chunk:
            body(0)
        else:
            lax.fori_loop(0, height // chunk, lambda i, c: (body(i * chunk), c)[1], 0)

    def image_row(i, count=1):
        start = i * width
        if not isinstance(start, int):
            start = pl.multiple_of(start, width)
        return pl.ds(start, count * width)

    def norm_terms(ref):
        def add(first):
            sums = []
            for i in range(chunk):
                part = ref[image_row(first + i), :].reshape(width // 8, 8, channels)
                sums.append((jnp.sum(part, axis=0), jnp.sum(part * part, axis=0)))
            while len(sums) > 1:
                pairs = [
                    (x[0] + y[0], x[1] + y[1]) for x, y in zip(sums[0::2], sums[1::2])
                ]
                sums = pairs + sums[2 * len(pairs) :]
            return sums[0]

        if height == chunk:
            sums = add(0)
        else:
            zero = jnp.zeros((8, channels), F32)

            def more(i, carry):
                part = add(i * chunk)
                return carry[0] + part[0], carry[1] + part[1]

            sums = lax.fori_loop(0, height // chunk, more, (zero, zero))
        row = lax.broadcasted_iota(jnp.int32, (16, channels), 0)
        stacked = jnp.zeros((16, channels), F32)
        for which, left in enumerate(sums):
            left = jnp.sum(left, axis=0, keepdims=True)
            for part, piece in enumerate(three_parts(left)):
                stacked = jnp.where(row == which * 3 + part, piece, stacked)
        totals = dot(stacked.astype(BF16), same_group)
        members = float(pixels * per_group)
        center = (totals[0:1] + totals[1:2] + totals[2:3]) / members
        square = (totals[3:4] + totals[4:5] + totals[5:6]) / members
        return center, lax.rsqrt(square - center * center + EPSILON)

    column = lax.broadcasted_iota(jnp.int32, (width, channels), 0)

    def fill_act(ref, terms):
        center, factor = terms

        def rows(first):
            for i in range(chunk):
                v = silu((ref[image_row(first + i), :] - center) * factor)
                before = jnp.where(column == 0, 0.0, pltpu.roll(v, 1, 0))
                after = jnp.where(column == width - 1, 0.0, pltpu.roll(v, width - 1, 0))
                taps = (before, v, after)
                wide = jnp.concatenate(
                    [t[:, 0:256] for t in taps]
                    + [t[:, 256:channels] for t in taps]
                    + [jnp.zeros((width, 1024 - 3 * channels), F32)],
                    axis=1,
                )
                high, low = split(wide)
                act_high[image_row(first + i + 1), :] = high
                act_low[image_row(first + i + 1), :] = low

        over_chunks(rows)

    half = chunk // 2 if chunk % 2 == 0 else chunk

    def convolve(high_ref, low_ref, add, beside=None):
        def depth(first, n):
            left = act_high[image_row(first, half), :]
            return (
                [left, act_low[image_row(first, half), :], left],
                [high_ref[n], high_ref[n], low_ref[n]],
            )

        def product(*terms):
            return dot(
                jnp.concatenate([x for left, _ in terms for x in left], axis=1),
                jnp.concatenate([x for _, right in terms for x in right], axis=0),
            )

        def rows(first):
            for i in range(0, chunk, half):
                at = first + i
                rest_ref[image_row(at + 1, half), :] = product(depth(at + 1, 3))
            for i in range(0, chunk, half):
                at = first + i
                total = product(depth(at, 0), depth(at + 1, 1), depth(at + 2, 2))
                place = image_row(at, half)
                value_ref[place, 0:256] = total + add(place)[:, 0:256]

        over_chunks(rows)
        if beside is not None:
            beside()

        def end(first):
            for i in range(chunk):
                place = image_row(first + i)
                total = add(place)[:, 256:channels]
                for a in range(3):
                    total = total + rest_ref[image_row(first + i + a), a * rest : (a + 1) * rest]
                value_ref[place, 256:channels] = total

        over_chunks(end)

    def project(high, low, values):
        vh, vl = split(values)
        both = dot(jnp.concatenate([high, low], axis=0), vh, NT)
        return both[0:32] + both[32:64] + dot(high, vl, NT)

    def level_copy(i, source, target, to):
        return pltpu.make_async_remote_copy(
            src_ref=source,
            dst_ref=target,
            send_sem=level_send.at[i],
            recv_sem=level_recv.at[i],
            device_id={"level": to},
            device_id_type=MESH,
        )

    wh, wm, wl = three_parts(w_in)
    w_in_parts = jnp.concatenate([wh, wm, wh, wm, wl, wh], axis=0).astype(BF16)

    def run_block(frame, beside=None):
        xh, xm, xl = three_parts(frame)
        left = jnp.concatenate([xh, xh, xm, xm, xh, xl], axis=0).T.astype(BF16)
        lifted_ref[...] = dot(left, w_in_parts)
        fill_act(lifted_ref, norm_terms(lifted_ref))
        convolve(first_high, first_low, lambda place: embedded, beside)
        fill_act(value_ref, norm_terms(value_ref))
        convolve(second_high, second_low, lambda place: lifted_ref[place, :])

    run_block(frame)
    hidden = value_ref[...]
    straight = project(w_out_high, w_out_low, hidden)[0:8]
    center, factor = norm_terms(value_ref)
    taps = project(folded_high, folded_low, silu((hidden - center) * factor))
    send_tap[...] = taps[0:4]
    frame_copy = level_copy(0, send_frame, recv_frame, level + 1)
    tap_copy = level_copy(1, send_tap, recv_tap, level + 2)
    pl.when(has_two_up)(lambda: tap_copy.start())
    send_frame[0:4, :] = (scale_x * frame + scale_noise * (straight + taps[8:16]))[0:4]
    send_frame[4:8, :] = jnp.broadcast_to(scale_noise, (4, pixels))
    pl.when(has_up)(lambda: frame_copy.start())
    pl.when(has_two_down)(lambda: tap_copy.wait_recv())
    pl.when(has_down)(lambda: frame_copy.wait_recv())
    moved = recv_frame[0:4, :] + recv_frame[4:8, :] * (recv_tap[...] + taps[16:20])
    moved = jnp.concatenate([moved, jnp.zeros((4, pixels), F32)], axis=0)
    frame = jnp.where(level == 0, entering, moved)
    pl.when(has_two_up)(lambda: tap_copy.wait_send())
    pl.when(has_up)(lambda: frame_copy.wait_send())

    run_block(frame)
    hidden = value_ref[pl.ds(pl.multiple_of(band * held, width), held), :]
    straight = project(w_out_high, w_out_low, hidden)[0:8]
    center, factor = norm_terms(value_ref)
    taps = project(folded_high, folded_low, silu((hidden - center) * factor))
    send_last[0] = taps[0:4]
    send_last[1] = taps[16:20]
    up_copy = level_copy(2, send_last.at[0], recv_last.at[0], level + 1)
    down_copy = level_copy(3, send_last.at[1], recv_last.at[1], level - 1)
    pl.when(has_up)(lambda: up_copy.start())
    pl.when(has_down)(lambda: down_copy.start())
    local = straight + taps[8:16]
    mine = frame[:, 0:held]
    for j in range(1, n_band):
        mine = jnp.where(band == j, frame[:, j * held : (j + 1) * held], mine)
    done = scale_x * mine + scale_noise * local
    for r in range(out_ref.shape[0]):
        out_ref[r] = done[0:lat, r * width : (r + 1) * width]
    pl.when(has_down)(lambda: up_copy.wait_recv())
    pl.when(has_up)(lambda: down_copy.wait_recv())
    late = scale_noise * (recv_last[0] + recv_last[1])
    for r in range(out_ref.shape[0]):
        late_ref[r] = late[0:lat, r * width : (r + 1) * width]
    pl.when(has_up)(lambda: up_copy.wait_send())
    pl.when(has_down)(lambda: down_copy.wait_send())


def on_device(
    mesh_sizes, latents, timesteps, fresh, w_in, conv_first, conv_second, w_time, temporal, w_out
):
    n_level, n_band = mesh_sizes
    lat, band_rows, width = latents.shape[1:]
    channels = w_in.shape[1]
    height = band_rows * n_band
    pixels = height * width
    held = band_rows * width
    chunk = max(d for d in range(1, 11) if height % d == 0)

    vmem = pl.BlockSpec(memory_space=pltpu.VMEM)
    hbm = pl.BlockSpec(memory_space=pl.ANY)
    sem = pltpu.SemaphoreType.DMA
    ready, late = pl.pallas_call(
        functools.partial(kernel, (n_level, n_band, channels, height, width, chunk)),
        out_shape=[jax.ShapeDtypeStruct((band_rows, lat, width), F32)] * 2,
        in_specs=[hbm] * 9,
        out_specs=[vmem] * 2,
        scratch_shapes=[
            pltpu.SMEM((1,), jnp.int32),
            *[pltpu.VMEM((band_rows, lat, width), F32)] * 2,
            *[pltpu.VMEM((lat, channels), F32)] * 2,
            pltpu.VMEM(conv_first.shape, F32),
            pltpu.VMEM(conv_second.shape, F32),
            pltpu.VMEM(w_time.shape, F32),
            pltpu.VMEM(temporal.shape, F32),
            *[pltpu.VMEM((4, 1024, 256), BF16)] * 4,
            *[pltpu.VMEM((pixels + 2 * width, 1024), BF16)] * 2,
            *[pltpu.VMEM((pixels, channels), F32)] * 2,
            pltpu.VMEM((pixels + 2 * width, 256), F32),
            pltpu.VMEM((16, held), F32),
            pltpu.VMEM((max(n_band - 1, 1), 16, held), F32),
            *[pltpu.VMEM((8, pixels), F32)] * 2,
            *[pltpu.VMEM((4, pixels), F32)] * 2,
            *[pltpu.VMEM((2, 4, held), F32)] * 2,
            sem((9,)),
            sem((max(n_band - 1, 1),)),
            sem((max(n_band - 1, 1),)),
            sem((4,)),
            sem((4,)),
        ],
        compiler_params=pltpu.CompilerParams(
            collective_id=0, has_side_effects=True, vmem_limit_bytes=60 * 1024 * 1024
        ),
    )(
        timesteps,
        latents[0].transpose(1, 0, 2),
        fresh[0].transpose(1, 0, 2),
        w_in,
        w_out.T,
        conv_first,
        conv_second,
        w_time,
        temporal,
    )
    return (ready + late).transpose(1, 0, 2)[None]


def solution(mesh):
    placed = (
        P("level", None, "band", None),
        P("level"),
        P(None, None, "band", None),
        P(),
        P(),
        P(),
        P(),
        P(),
        P(),
    )
    return jax.shard_map(
        functools.partial(on_device, (mesh.shape["level"], mesh.shape["band"])),
        mesh=mesh,
        in_specs=placed,
        out_specs=P("level", None, "band", None),
        check_vma=False,
    )
```
